256 devices in a mesh: tm: 8 (over y, x_hi), strip: 32 (over z, x_lo, core).
Axes of the slice: x: 4 (x_hi: 2, x_lo: 2; x = x_hi * 2 + x_lo), y: 4, z: 8, core: 2. Of those that a mesh axis runs over, the one named last changes fastest.
Arguments:
- video: bfloat16 [16, 128, 512, 256], P('tm', 'strip'), may hold values from -6 to 6
- gain_one: float32 [256], replicated, may hold values from 0.25 to 1.75
- conv_one: bfloat16 [3, 3, 256, 256], replicated, may hold values from -0.125 to 0.125
- gain_two: float32 [256], replicated, may hold values from 0.25 to 1.75
- conv_two: bfloat16 [3, 3, 256, 256], replicated, may hold values from -0.125 to 0.125
- gain_three: float32 [256], replicated, may hold values from 0.25 to 1.75
- time_kernel: bfloat16 [3, 256, 256], replicated, may hold values from -0.21875 to 0.21875
- gain_four: float32 [256], replicated, may hold values from 0.25 to 1.75
- query_weight: bfloat16 [256, 256], replicated
- key_weight: bfloat16 [256, 256], replicated
- value_weight: bfloat16 [256, 256], replicated, may hold values from -0.375 to 0.375
- out_weight: bfloat16 [256, 256], replicated, may hold values from -0.375 to 0.375
Outputs:
- encoded: bfloat16 [16, 128, 512, 256], P('tm', 'strip')
The draws below stay inside these ranges and needn't reach their ends.
All inputs are finite; a program needn't handle non-finite values.
Results may differ from the reference program's by a relative error of at most 0.015.
Values may be sent and summed in bfloat16 or wider, within the bound.
No kernel may reach another device: no remote copies, remote signals or barrier semaphores. Data moves between devices by JAX's collectives and lax.ppermute only.
A program may use at most 128 MiB of HBM per device.

```python
import jax
import jax.numpy as jnp
from jax import lax

C = 256
COLS = 512
TIME = 16
HEIGHT = 128


def shared_part(key):
    return jax.random.normal(key, (C, C), jnp.float32)


def projection(key, common, mixing):
    own = jax.random.normal(key, (C, C), jnp.float32)
    return (mixing * common + own) / jnp.sqrt(jnp.float32(C) * (1.0 + mixing * mixing)) * jnp.sqrt(1.0 + mixing * mixing)


def draw_query_weight(key, part):
    common = shared_part(key)
    key = jax.random.fold_in(key, 11)
    mixing = 0.6
    return projection(key, common, mixing).astype(jnp.bfloat16)


def draw_key_weight(key, part):
    common = shared_part(key)
    key = jax.random.fold_in(key, 23)
    mixing = 0.6
    return projection(key, common, mixing).astype(jnp.bfloat16)


def levels(key, extent, pieces, smallest, largest):
    level = 1.0
    for position, shards_of in pieces:
        heights = jax.random.uniform(jax.random.fold_in(jax.random.fold_in(key, 6), position), (shards_of,), jnp.float32, smallest / len(pieces), largest / len(pieces))
        level = level * jnp.repeat(jnp.exp(heights), extent[position] // shards_of).reshape((-1,) + (1,) * (len(extent) - 1 - position))
    return level


def bell_draw(stream_key, extent, deviation, bound, pieces=(), kind=jnp.bfloat16):
    level = levels(stream_key, extent, pieces, -0.22, 0.18) if pieces else 1.0
    entries = jax.random.normal(stream_key, extent, jnp.float32) * deviation * level
    return jnp.minimum(jnp.maximum(entries, -bound), bound).astype(kind)


def setup_inputs(seed: int = 0) -> dict:
    arg_keys = jax.random.split(jax.random.key(seed), 13)
    video = bell_draw(arg_keys[0], (TIME, HEIGHT, COLS, C), 1.0, 6.0, ((0, 8), (1, 32)))
    gain_one = jnp.clip(1.0 + 0.15 * jax.random.normal(arg_keys[1], (C,), jnp.float32), 0.25, 1.75)
    conv_one = bell_draw(arg_keys[2], (3, 3, C, C), (9 * C) ** -0.5, 0.125)
    gain_two = jnp.clip(1.0 + 0.15 * jax.random.normal(arg_keys[3], (C,), jnp.float32), 0.25, 1.75)
    conv_two = bell_draw(arg_keys[4], (3, 3, C, C), (9 * C) ** -0.5, 0.125)
    gain_three = jnp.clip(1.0 + 0.15 * jax.random.normal(arg_keys[5], (C,), jnp.float32), 0.25, 1.75)
    time_kernel = bell_draw(arg_keys[6], (3, C, C), (3 * C) ** -0.5, 0.21875)
    gain_four = jnp.clip(1.0 + 0.15 * jax.random.normal(arg_keys[7], (C,), jnp.float32), 0.25, 1.75)
    query_weight = draw_query_weight(jax.random.fold_in(arg_keys[12], 71), 0)
    key_weight = draw_key_weight(jax.random.fold_in(arg_keys[12], 71), 0)
    value_weight = bell_draw(arg_keys[10], (C, C), C ** -0.5, 0.375)
    out_weight = bell_draw(arg_keys[11], (C, C), C ** -0.5, 0.375)
    return {"video": video, "gain_one": gain_one, "conv_one": conv_one, "gain_two": gain_two, "conv_two": conv_two, "gain_three": gain_three, "time_kernel": time_kernel, "gain_four": gain_four, "query_weight": query_weight, "key_weight": key_weight, "value_weight": value_weight, "out_weight": out_weight}


def normalize(values, gain):
    values = values.astype(jnp.float32)
    return values * lax.rsqrt(lax.optimization_barrier(jnp.mean(values * values, axis=-1, keepdims=True)) + 1e-06) * gain

def spatial(padded_rows, kernel):
    padded = jnp.pad(padded_rows, ((0, 0), (0, 0), (1, 1), (0, 0)))
    rows = padded.shape[1] - 2
    cols = padded.shape[2] - 2
    total = jnp.zeros((padded.shape[0], rows, cols, kernel.shape[3]), jnp.float32)
    for i in range(3):
        for j in range(3):
            piece = padded[:, i:i + rows, j:j + cols, :]
            total = total + jnp.dot(piece, kernel[i, j], preferred_element_type=jnp.float32)
    return total

def reference(video, gain_one, conv_one, gain_two, conv_two, gain_three, time_kernel, gain_four, query_weight, key_weight, value_weight, out_weight):
    rowpad = ((0, 0), (1, 1), (0, 0), (0, 0))
    first = jax.nn.silu(normalize(video, gain_one)).astype(jnp.bfloat16)
    hidden = spatial(jnp.pad(first, rowpad), conv_one).astype(jnp.bfloat16)
    second = jax.nn.silu(normalize(hidden, gain_two)).astype(jnp.bfloat16)
    mixed = (video.astype(jnp.float32) + spatial(jnp.pad(second, rowpad), conv_two)).astype(jnp.bfloat16)
    third = jax.nn.silu(normalize(mixed, gain_three)).astype(jnp.bfloat16)
    back_one = jnp.concatenate([third[:1], third[:-1]], axis=0)
    back_two = jnp.concatenate([third[:1], third[:1], third[:-2]], axis=0)
    change = jnp.dot(back_two, time_kernel[0], preferred_element_type=jnp.float32)
    change = change + jnp.dot(back_one, time_kernel[1], preferred_element_type=jnp.float32)
    change = change + jnp.dot(third, time_kernel[2], preferred_element_type=jnp.float32)
    timed = (mixed.astype(jnp.float32) + change).astype(jnp.bfloat16)
    fourth = normalize(timed, gain_four).astype(jnp.bfloat16)
    queries = jnp.dot(fourth, query_weight, preferred_element_type=jnp.float32).astype(jnp.bfloat16)
    keys = jnp.dot(fourth, key_weight, preferred_element_type=jnp.float32).astype(jnp.bfloat16)
    values = jnp.dot(fourth, value_weight, preferred_element_type=jnp.float32).astype(jnp.bfloat16)
    frames = video.shape[0]
    causal = jnp.arange(frames)[:, None] >= jnp.arange(frames)[None, :]

    def one_row(row):
        qrow = queries[:, row].astype(jnp.float32)
        krow = keys[:, row].astype(jnp.float32)
        vrow = values[:, row].astype(jnp.float32)
        scores = jnp.einsum('twc,swc->wts', qrow, krow) / jnp.sqrt(jnp.float32(C))
        scores = jnp.where(causal[None], scores, -1e+30)
        weights = jax.nn.softmax(scores, axis=-1).astype(jnp.bfloat16)
        return jnp.einsum('wts,swc->twc', weights.astype(jnp.float32), vrow).astype(jnp.bfloat16)
    attended = lax.map(one_row, jnp.arange(video.shape[1]))
    attended = jnp.transpose(attended, (1, 0, 2, 3))
    final = timed.astype(jnp.float32) + jnp.dot(attended, out_weight, preferred_element_type=jnp.float32)
    return final.astype(jnp.bfloat16)
```

```python
import functools

import jax
import jax.numpy as jnp
from jax import lax
from jax.experimental import pallas as pl
from jax.experimental.pallas import tpu as pltpu
from jax.sharding import PartitionSpec as P

BF16 = jnp.bfloat16
F32 = jnp.float32
EDGE = 16
EPS = 1e-06


def scaled(values, gain):
    mean = jnp.mean(values * values, axis=-1, keepdims=True)
    return values * lax.rsqrt(mean + EPS) * gain


def silu_from_half(half):
    return half + half * jnp.tanh(half)


def put_shifted(dst, row, values):
    width, chans = values.shape
    index = lax.broadcasted_iota(jnp.int32, (width, 1), 0)
    before = jnp.where(index == 0, 0.0, pltpu.roll(values, 1, 0))
    after = jnp.where(index == width - 1, 0.0, pltpu.roll(values, width - 1, 0))
    dst[row, :, 0:chans] = before.astype(BF16)
    dst[row, :, chans : 2 * chans] = values.astype(BF16)
    dst[row, :, 2 * chans : 3 * chans] = after.astype(BF16)


def conv_body(plan, flags, video, *refs):
    (window, keep, parts, owners, rows) = plan
    halos, (gain_one, conv_one, gain_two, conv_two, out, s_one, s_two) = refs[:-7], refs[-7:]
    start, stop = window
    width = stop - start
    half_one = gain_one[...] * 0.5
    half_two = gain_two[...] * 0.5
    chans = gain_one.shape[-1]

    def halo_row(side, row):
        pieces = []
        for number, (low, high) in enumerate(parts):
            a, b = max(low, start), min(high, stop)
            if a < b:
                pieces.append(halos[2 * number + side][0, row, a - low : b - low, :])
        return pieces[0] if len(pieces) == 1 else jnp.concatenate(pieces, axis=0)

    for row in range(rows + 4):
        if row < 2:
            raw = halo_row(0, row)
        elif row < rows + 2:
            raw = video[0, row - 2, start:stop, :]
        else:
            raw = halo_row(1, row - rows - 2)
        put_shifted(s_one, row, silu_from_half(scaled(raw.astype(F32), half_one)))

    def product(source, weights, row):
        lhs = jnp.concatenate([source[row + i] for i in range(3)], axis=-1)
        return jnp.dot(lhs, weights[...], preferred_element_type=F32)

    for row in range(rows + 2):
        hidden = product(s_one, conv_one, row)
        second = silu_from_half(scaled(hidden, half_two))
        if row == 0:
            second = second * flags[0]
        if row == rows + 1:
            second = second * flags[1]
        put_shifted(s_two, row, second)

    low, high = keep[0] - start, keep[1] - start
    for row in range(rows):
        change = product(s_two, conv_two, row)[low:high]
        base = video[0, row, keep[0] : keep[1], :].astype(F32)
        mixed = (base + change).astype(BF16)
        out[:, 0, row] = mixed.reshape(owners, (high - low) // owners, chans)


def conv_chunk(video, flags, halos, parts, window, keep, owners, weights):
    frames, rows, cols, chans = video.shape
    gain_one, conv_one, gain_two, conv_two = weights
    width = window[1] - window[0]
    own = (keep[1] - keep[0]) // owners
    plan = (window, keep, parts, owners, rows)
    whole = lambda shape: pl.BlockSpec(shape, lambda f: (0,) * len(shape))
    halo_specs = [
        pl.BlockSpec((1,) + h.shape[1:], lambda f: (f, 0, 0, 0)) for h in halos
    ]
    flops = 2 * frames * (2 * rows + 2) * width * 9 * chans * chans
    return pl.pallas_call(
        functools.partial(conv_body, plan),
        grid=(frames,),
        in_specs=[
            pl.BlockSpec(memory_space=pltpu.SMEM),
            pl.BlockSpec((1, rows, cols, chans), lambda f: (f, 0, 0, 0)),
            *halo_specs,
            whole((1, chans)),
            whole((9 * chans, chans)),
            whole((1, chans)),
            whole((9 * chans, chans)),
        ],
        out_specs=pl.BlockSpec((owners, 1, rows, own, chans), lambda f: (0, f, 0, 0, 0)),
        out_shape=jax.ShapeDtypeStruct((owners, frames, rows, own, chans), BF16),
        scratch_shapes=[
            pltpu.VMEM((rows + 4, width, 3 * chans), BF16),
            pltpu.VMEM((rows + 2, width, 3 * chans), BF16),
        ],
        compiler_params=pltpu.CompilerParams(vmem_limit_bytes=40 * 1024 * 1024),
        cost_estimate=pl.CostEstimate(flops=flops, bytes_accessed=8 * 1024 * 1024, transcendentals=0),
        name="convs",
    )(flags, video, *halos, gain_one, conv_one, gain_two, conv_two)


def attend_body(group, x_ref, gain_three, kernel, gain_four, wq, wk, wv, wo, out_ref):
    frames, pixels, chans = x_ref.shape
    count = frames * pixels
    half_three = gain_three[...] * 0.5
    x = x_ref[...].reshape(count, chans).astype(F32)
    third = silu_from_half(scaled(x, half_three)).astype(BF16).reshape(frames, pixels, chans)
    one = jnp.concatenate([third[:1], third[:-1]], axis=0)
    two = jnp.concatenate([third[:1], third[:1], third[:-2]], axis=0)
    taps = jnp.concatenate([two, one, third], axis=-1).reshape(count, 3 * chans)
    timed = x + jnp.dot(taps, kernel[...], preferred_element_type=F32)
    fourth = scaled(timed, gain_four[...]).astype(BF16)
    project = lambda w: jnp.dot(fourth, w[...], preferred_element_type=F32)
    scale = 1.0 / float(chans) ** 0.5
    queries = (project(wq) * scale).astype(BF16).reshape(frames, pixels, chans)
    keys = project(wk).astype(BF16).reshape(frames, pixels, chans)
    values = project(wv).astype(BF16).reshape(frames, pixels, chans)
    size = frames * group
    down = lax.broadcasted_iota(jnp.int32, (size, size), 0)
    along = lax.broadcasted_iota(jnp.int32, (size, size), 1)
    allowed = (down % group == along % group) & (down >= along)
    pieces = []
    for g in range(pixels // group):
        cut = lambda v: v[:, g * group : (g + 1) * group].reshape(size, chans)
        scores = lax.dot_general(
            cut(queries), cut(keys), (((1,), (1,)), ((), ())), preferred_element_type=F32
        )
        scores = jnp.where(allowed, scores, -1e30)
        top = jnp.max(scores, axis=-1, keepdims=True)
        weights = jnp.exp(scores - top)
        total = jnp.sum(weights, axis=-1, keepdims=True)
        weights = (weights * (1.0 / total)).astype(BF16)
        attended = jnp.dot(weights, cut(values), preferred_element_type=F32)
        pieces.append(attended.astype(BF16).reshape(frames, group, chans))
    attended = pieces[0] if len(pieces) == 1 else jnp.concatenate(pieces, axis=1)
    final = timed + jnp.dot(
        attended.reshape(count, chans), wo[...], preferred_element_type=F32
    )
    out_ref[...] = final.astype(BF16).reshape(frames, pixels, chans)


def attend_chunk(x, weights, tile, group):
    frames, pixels, chans = x.shape
    tile = min(tile, pixels)
    whole = lambda a: pl.BlockSpec(a.shape, lambda p: (0,) * a.ndim)
    spec = pl.BlockSpec((frames, tile, chans), lambda p: (0, p, 0))
    return pl.pallas_call(
        functools.partial(attend_body, group),
        grid=(pixels // tile,),
        in_specs=[spec] + [whole(w) for w in weights],
        out_specs=spec,
        out_shape=jax.ShapeDtypeStruct(x.shape, BF16),
        compiler_params=pltpu.CompilerParams(vmem_limit_bytes=40 * 1024 * 1024),
        cost_estimate=pl.CostEstimate(
            flops=2 * frames * pixels * chans * chans * 9,
            bytes_accessed=4 * 1024 * 1024,
            transcendentals=0,
        ),
        name="attend",
    )(x, *weights)


def shards(
    video,
    gain_one,
    conv_one,
    gain_two,
    conv_two,
    gain_three,
    time_kernel,
    gain_four,
    query_weight,
    key_weight,
    value_weight,
    out_weight,
):
    frames, rows, cols, chans = video.shape
    owners = lax.axis_size("tm")
    strips = lax.axis_size("strip")
    strip = lax.axis_index("strip")
    chunks = 2
    step = cols // chunks
    forward = [(i, i + 1) for i in range(strips - 1)]
    backward = [(i + 1, i) for i in range(strips - 1)]
    flags = jnp.stack([strip > 0, strip < strips - 1]).astype(F32)
    row = lambda gain: gain.reshape(1, chans)
    flat = lambda w: w.reshape(-1, chans)
    conv_weights = (row(gain_one), flat(conv_one), row(gain_two), flat(conv_two))
    attend_weights = (
        row(gain_three), flat(time_kernel), row(gain_four),
        query_weight, key_weight, value_weight, out_weight,
    )

    edges = [0] + [min(step * (c + 1) + EDGE, cols) for c in range(chunks)]
    parts = [(edges[c], edges[c + 1]) for c in range(chunks)]
    halos = []
    for low, high in parts:
        halos.append(lax.ppermute(video[:, rows - 2 :, low:high], "strip", forward))
        halos.append(lax.ppermute(video[:, :2, low:high], "strip", backward))

    outs = []
    for c in range(chunks):
        keep = (c * step, (c + 1) * step)
        window = (max(keep[0] - EDGE, 0), min(keep[1] + EDGE, cols))
        used = [n for n, (low, high) in enumerate(parts) if low < window[1] and high > window[0]]
        mixed = conv_chunk(
            video, flags, [halos[2 * n + s] for n in used for s in (0, 1)],
            [parts[n] for n in used], window, keep, owners, conv_weights,
        )
        block = lax.all_to_all(mixed, "tm", split_axis=0, concat_axis=0, tiled=True)
        own = step // owners
        final = attend_chunk(
            block.reshape(owners * frames, rows * own, chans), attend_weights, 64, 16
        )
        final = final.reshape(owners, frames, rows, own, chans)
        back = lax.all_to_all(final, "tm", split_axis=0, concat_axis=0, tiled=True)
        outs.append(jnp.transpose(back, (1, 2, 0, 3, 4)).reshape(frames, rows, step, chans))
    return jnp.concatenate(outs, axis=2)


def solution(mesh):
    placed = (P("tm", "strip", None, None), P(), P(), P(), P(), P(), P(), P(), P(), P(), P(), P())
    return jax.shard_map(
        shards, mesh=mesh, in_specs=placed, out_specs=P("tm", "strip", None, None), check_vma=False
    )
```

```python
import functools

import jax
import jax.numpy as jnp
from jax import lax
from jax.experimental import pallas as pl
from jax.experimental.pallas import tpu as pltpu
from jax.sharding import PartitionSpec as P

BF16 = jnp.bfloat16
F32 = jnp.float32
EPS = 1e-06
HALF = 2


def scaled(values, gain):
    mean = jnp.mean(values * values, axis=-1, keepdims=True)
    return values * lax.rsqrt(mean + EPS) * gain


def silu_from_half(half):
    return half + half * jnp.tanh(half)


def put_shifted(dst, row, values):
    width, chans = values.shape
    index = lax.broadcasted_iota(jnp.int32, (width, 1), 0)
    before = jnp.where(index == 0, 0.0, pltpu.roll(values, 1, 0))
    after = jnp.where(index == width - 1, 0.0, pltpu.roll(values, width - 1, 0))
    dst[row, :, 0:chans] = before.astype(BF16)
    dst[row, :, chans : 2 * chans] = values.astype(BF16)
    dst[row, :, 2 * chans : 3 * chans] = after.astype(BF16)


def product(source, weights, row):
    lhs = jnp.concatenate([source[row + i] for i in range(3)], axis=-1)
    return jnp.dot(lhs, weights[...], preferred_element_type=F32)


def send(base, change, frame, index, held, out, sems):
    mixed = (base.astype(F32) + change).astype(BF16)
    held[frame, index] = mixed.reshape(held.shape[2:])
    copy = pltpu.make_async_copy(
        held.at[frame, index], out.at[:, frame, index], sems.at[frame, index]
    )
    copy.start()
    return copy


def inner_body(info, inner, outer, halo, gain_one, w_one, gain_two, conv_two,
               out, shared, s_one, s_two, w_two, kept, held, w_sem, kept_sems, sems):
    frames, _, width, chans = inner.shape
    odd = info[0] == 1
    half_one = gain_one[...] * 0.5
    half_two = gain_two[...] * 0.5
    load = pltpu.make_async_copy(conv_two, w_two, w_sem)
    load.start()

    def put_first(frame, index):
        if index < HALF:
            raw = jnp.where(odd, halo[frame, index], outer[frame, index])
        elif index < 2 * HALF:
            raw = inner[frame, index - HALF]
        else:
            raw = jnp.where(odd, outer[frame, index - 2 * HALF], halo[frame, index - 2 * HALF])
        put_shifted(s_one.at[frame], index, silu_from_half(scaled(raw.astype(F32), half_one)))

    def put_second(frame, index):
        hidden = product(s_one.at[frame], w_one, index)
        put_shifted(s_two.at[frame], index, silu_from_half(scaled(hidden, half_two)))

    for index in range(3 * HALF):
        put_first(0, index)
    copies = []
    for frame in range(frames):
        for index in range(2 * HALF):
            if frame + 1 < frames:
                for ahead in range(index * 3 // 2, (index + 1) * 3 // 2):
                    put_first(frame + 1, ahead)
            put_second(frame, index)
    load.wait()
    for frame in range(frames):
        here = slice(chans, 2 * chans)
        for index in range(HALF):
            kept[frame, index] = jnp.where(
                odd, s_two[frame, HALF + index, :, here], s_two[frame, index, :, here]
            )
        copy = pltpu.make_async_copy(kept.at[frame], shared.at[frame], kept_sems.at[frame])
        copy.start()
        copies.append(copy)
        for index in range(HALF):
            change = product(s_two.at[frame], w_two, index)
            copies.append(send(inner[frame, index], change, frame, index, held, out, sems))
    for copy in copies:
        copy.wait()


def outer_body(info, outer, halo, shared, gain_one, w_one, gain_two, conv_two,
               out, s_one, s_two_a, s_two_b, w_two, kept, held, w_sem, kept_sems, sems):
    frames, _, width, chans = outer.shape
    odd, goes_on = info[0] == 1, info[1] == 1
    new_at = jnp.where(odd, HALF, 0)
    shared_at = HALF - new_at
    half_one = gain_one[...] * 0.5
    half_two = gain_two[...] * 0.5
    s_two = (s_two_a, s_two_b)
    fetch = pltpu.make_async_copy(shared, kept, kept_sems.at[0])
    load = pltpu.make_async_copy(conv_two, w_two, w_sem)
    fetch.start()
    load.start()

    def put_first(frame, index):
        if index < HALF:
            raw = jnp.where(odd, outer[frame, index], halo[frame, index])
        else:
            raw = jnp.where(odd, halo[frame, index - HALF], outer[frame, index - HALF])
        put_shifted(s_one.at[frame], index, silu_from_half(scaled(raw.astype(F32), half_one)))

    def put_second(frame, index):
        hidden = product(s_one.at[frame], w_one, index)
        second = silu_from_half(scaled(hidden, half_two))
        outside = jnp.logical_not(goes_on) & (odd if index == HALF - 1 else jnp.logical_not(odd))
        second = jnp.where(outside, 0.0, second)
        put_shifted(s_two[frame], new_at + index, second)

    for index in range(2 * HALF):
        put_first(0, index)
    for frame in range(frames):
        for index in range(HALF):
            if frame + 1 < frames:
                for ahead in range(2 * index, 2 * index + 2):
                    put_first(frame + 1, ahead)
            put_second(frame, index)
        if frame == 0:
            fetch.wait()
            load.wait()
        for index in range(HALF):
            put_shifted(s_two[frame], shared_at + index, kept[frame, index].astype(F32))
    copies = []
    for frame in range(frames):
        for index in range(HALF):
            change = product(s_two[frame], w_two, index)
            copies.append(send(outer[frame, index], change, frame, index, held, out, sems))
    for copy in copies:
        copy.wait()


def conv_chunk(info, inner, outer, halo, shared, owners, weights):
    frames, _, cols, chans = outer.shape
    own = cols // owners
    is_outer = shared is not None
    stack = lambda count: pltpu.VMEM((frames, count, cols, 3 * chans), BF16)
    here = pl.BlockSpec(memory_space=pltpu.VMEM)
    there = pl.BlockSpec(memory_space=pltpu.HBM)
    near = lambda v: pltpu.with_memory_space_constraint(v, pltpu.VMEM)
    far = lambda v: pltpu.with_memory_space_constraint(v, pltpu.HBM)
    gain_one, conv_one, gain_two, conv_two = weights
    mixed = pltpu.HBM((owners, frames, HALF, own, chans), BF16)
    keep = pltpu.HBM((frames, HALF, cols, chans), BF16)
    first_rows = (2 if is_outer else 3) * HALF
    new_rows = (1 if is_outer else 2) * HALF
    flops = 2 * frames * (new_rows + HALF) * cols * 9 * chans * chans
    two = [pltpu.VMEM((2 * HALF, cols, 3 * chans), BF16)] * 2 if is_outer else [stack(2 * HALF)]
    return pl.pallas_call(
        outer_body if is_outer else inner_body,
        in_specs=[
            pl.BlockSpec(memory_space=pltpu.SMEM), here, here, there if is_outer else here,
            here, here, here, there,
        ],
        out_specs=[there] if is_outer else [there, there],
        out_shape=[mixed] if is_outer else [mixed, keep],
        scratch_shapes=[
            stack(first_rows),
            *two,
            pltpu.VMEM(conv_two.shape, BF16),
            pltpu.VMEM((frames, HALF, cols, chans), BF16),
            pltpu.VMEM((frames, HALF, owners, own, chans), BF16),
            pltpu.SemaphoreType.DMA,
            pltpu.SemaphoreType.DMA((frames,)),
            pltpu.SemaphoreType.DMA((frames, HALF)),
        ],
        compiler_params=pltpu.CompilerParams(vmem_limit_bytes=28 * 1024 * 1024),
        cost_estimate=pl.CostEstimate(
            flops=flops, bytes_accessed=8 * 1024 * 1024, transcendentals=0
        ),
        name="convs_outer" if is_outer else "convs_inner",
    )(
        info, *((outer, halo, far(shared)) if is_outer else (inner, outer, halo)),
        gain_one, near(conv_one), gain_two, far(conv_two),
    )


def attend_body(group, x_ref, gain_three, kernel, gain_four, wq, wk, wv, wo, *refs):
    out_ref = refs[-1]
    frames, pixels, chans = x_ref.shape
    count = frames * pixels
    half_three = gain_three[...] * 0.5
    x = x_ref[...].reshape(count, chans).astype(F32)
    third = silu_from_half(scaled(x, half_three)).astype(BF16).reshape(frames, pixels, chans)
    one = jnp.concatenate([third[:1], third[:-1]], axis=0)
    two = jnp.concatenate([third[:1], third[:1], third[:-2]], axis=0)
    taps = jnp.concatenate([two, one, third], axis=-1).reshape(count, 3 * chans)
    timed = x + jnp.dot(taps, kernel[...], preferred_element_type=F32)
    fourth = scaled(timed, gain_four[...]).astype(BF16)
    project = lambda w: jnp.dot(fourth, w[...], preferred_element_type=F32)
    scale = 1.0 / float(chans) ** 0.5
    queries = (project(wq) * scale).astype(BF16).reshape(frames, pixels, chans)
    keys = project(wk).astype(BF16).reshape(frames, pixels, chans)
    values = project(wv).astype(BF16).reshape(frames, pixels, chans)
    size = frames * group
    down = lax.broadcasted_iota(jnp.int32, (size, size), 0)
    along = lax.broadcasted_iota(jnp.int32, (size, size), 1)
    allowed = (down % group == along % group) & (down >= along)
    pieces = []
    for g in range(pixels // group):
        cut = lambda v: v[:, g * group : (g + 1) * group].reshape(size, chans)
        scores = lax.dot_general(
            cut(queries), cut(keys), (((1,), (1,)), ((), ())), preferred_element_type=F32
        )
        scores = jnp.where(allowed, scores, -1e30)
        top = jnp.max(scores, axis=-1, keepdims=True)
        weights = jnp.exp(scores - top)
        total = jnp.sum(weights, axis=-1, keepdims=True)
        weights = (weights * (1.0 / total)).astype(BF16)
        attended = jnp.dot(weights, cut(values), preferred_element_type=F32)
        pieces.append(attended.astype(BF16).reshape(frames, group, chans))
    attended = pieces[0] if len(pieces) == 1 else jnp.concatenate(pieces, axis=1)
    final = timed + jnp.dot(
        attended.reshape(count, chans), wo[...], preferred_element_type=F32
    )
    out_ref[...] = final.astype(BF16).reshape(frames, pixels, chans)


def attend_chunk(x, weights, tile, group, result=None):
    frames, pixels, chans = x.shape
    tile = min(tile, pixels)
    skip = 0 if result is None else pixels // tile
    given = [] if result is None else [result]
    far = lambda v: pltpu.with_memory_space_constraint(v, pltpu.HBM)
    whole = lambda a: pl.BlockSpec(a.shape, lambda p: (0,) * a.ndim)
    return pl.pallas_call(
        functools.partial(attend_body, group),
        grid=(pixels // tile,),
        in_specs=[pl.BlockSpec((frames, tile, chans), lambda p: (0, p, 0))]
        + [whole(w) for w in weights]
        + [pl.BlockSpec(memory_space=pltpu.HBM)] * len(given),
        out_specs=pl.BlockSpec((frames, tile, chans), lambda p: (0, p + skip, 0)),
        out_shape=pltpu.HBM((frames, 2 * pixels, chans), BF16),
        input_output_aliases={1 + len(weights): 0} if given else {},
        compiler_params=pltpu.CompilerParams(vmem_limit_bytes=32 * 1024 * 1024),
        cost_estimate=pl.CostEstimate(
            flops=2 * frames * pixels * chans * chans * 9,
            bytes_accessed=4 * 1024 * 1024,
            transcendentals=0,
        ),
        name="attend",
    )(x, *[w if w.shape[0] == 1 else far(w) for w in weights], *given)


def place_body(starts, back, out, sems):
    owners, _, parts, rows, own, _ = back.shape
    copies = [
        pltpu.make_async_copy(
            back.at[o, :, n],
            out.at[:, pl.ds(starts[n], rows), pl.ds(o * own, own)],
            sems.at[n, o],
        )
        for o in range(owners)
        for n in range(parts)
    ]
    for copy in copies:
        copy.start()
    for copy in copies:
        copy.wait()


def place(starts, back, shape):
    owners, _, parts = back.shape[:3]
    return pl.pallas_call(
        place_body,
        in_specs=[
            pl.BlockSpec(memory_space=pltpu.SMEM), pl.BlockSpec(memory_space=pltpu.VMEM),
        ],
        out_specs=pl.BlockSpec(memory_space=pltpu.HBM),
        out_shape=pltpu.HBM(shape, BF16),
        scratch_shapes=[pltpu.SemaphoreType.DMA((parts, owners))],
        compiler_params=pltpu.CompilerParams(vmem_limit_bytes=16 * 1024 * 1024),
        cost_estimate=pl.CostEstimate(
            flops=0, bytes_accessed=4 * 1024 * 1024, transcendentals=0
        ),
        name="place",
    )(starts, back)


def split_body(starts, video, inner, outer, sems):
    copies = [
        pltpu.make_async_copy(video.at[:, pl.ds(starts[n], HALF)], part, sems.at[n])
        for n, part in ((1, outer), (0, inner))
    ]
    for copy in copies:
        copy.start()
    for copy in copies:
        copy.wait()


def split(starts, video):
    frames, rows, cols, chans = video.shape
    part = jax.ShapeDtypeStruct((frames, HALF, cols, chans), BF16)
    here = pl.BlockSpec(memory_space=pltpu.VMEM)
    return pl.pallas_call(
        split_body,
        in_specs=[
            pl.BlockSpec(memory_space=pltpu.SMEM), pl.BlockSpec(memory_space=pltpu.HBM),
        ],
        out_specs=[here, here],
        out_shape=[part, part],
        scratch_shapes=[pltpu.SemaphoreType.DMA((2,))],
        compiler_params=pltpu.CompilerParams(vmem_limit_bytes=8 * 1024 * 1024),
        cost_estimate=pl.CostEstimate(
            flops=0, bytes_accessed=4 * 1024 * 1024, transcendentals=0
        ),
        name="split",
    )(starts, pltpu.with_memory_space_constraint(video, pltpu.HBM))


def shards(
    video,
    gain_one,
    conv_one,
    gain_two,
    conv_two,
    gain_three,
    time_kernel,
    gain_four,
    query_weight,
    key_weight,
    value_weight,
    out_weight,
):
    owners = lax.axis_size("tm")
    strips = lax.axis_size("strip")
    strip = lax.axis_index("strip")
    chans = video.shape[-1]
    odd = strip % 2
    siblings = [(i, i ^ 1) for i in range(strips)]
    neighbours = [(i, i + 1 if i % 2 else i - 1) for i in range(1, strips - 1)]
    inner_start = HALF - HALF * odd
    outer_start = HALF * odd
    goes_on = (strip > 0) & (strip < strips - 1)
    info = jnp.stack([odd, goes_on.astype(jnp.int32)])
    row = lambda gain: gain.reshape(1, chans)
    flat = lambda w: w.reshape(-1, chans)
    conv_weights = (row(gain_one), flat(conv_one), row(gain_two), flat(conv_two))
    attend_weights = (
        row(gain_three), flat(time_kernel), row(gain_four),
        query_weight, key_weight, value_weight, out_weight,
    )
    starts = jnp.stack([inner_start, outer_start])
    inner, outer = split(starts, video)
    from_outer = lax.ppermute(outer, "strip", neighbours)
    from_sibling = lax.ppermute(inner, "strip", siblings)

    final = shared = None
    for halo in (from_sibling, from_outer):
        mixed, *kept = conv_chunk(info, inner, outer, halo, shared, owners, conv_weights)
        shared = kept[0] if kept else None
        block = lax.all_to_all(mixed, "tm", split_axis=0, concat_axis=0, tiled=True)
        frames = block.shape[0] * block.shape[1]
        final = attend_chunk(block.reshape(frames, -1, chans), attend_weights, 64, 16, final)
    final = final.reshape(owners, block.shape[1], 2, *block.shape[2:])
    back = lax.all_to_all(final, "tm", split_axis=0, concat_axis=0, tiled=True)
    return place(starts, back, video.shape)


def solution(mesh):
    placed = (P("tm", "strip", None, None), P(), P(), P(), P(), P(), P(), P(), P(), P(), P(), P())
    return jax.shard_map(
        shards, mesh=mesh, in_specs=placed, out_specs=P("tm", "strip", None, None), check_vma=False
    )
```

```python
import functools

import jax
import jax.numpy as jnp
from jax import lax
from jax.experimental import pallas as pl
from jax.experimental.pallas import tpu as pltpu
from jax.sharding import PartitionSpec as P

BF16 = jnp.bfloat16
F32 = jnp.float32
EPS = 1e-06
HALF = 2


def scaled(values, gain):
    mean = jnp.mean(values * values, axis=-1, keepdims=True)
    return values * lax.rsqrt(mean + EPS) * gain


def silu_from_half(half):
    return half + half * jnp.tanh(half)


def put_shifted(dst, row, values):
    width, chans = values.shape
    index = lax.broadcasted_iota(jnp.int32, (width, 1), 0)
    before = jnp.where(index == 0, 0.0, pltpu.roll(values, 1, 0))
    after = jnp.where(index == width - 1, 0.0, pltpu.roll(values, width - 1, 0))
    dst[row, :, 0:chans] = before.astype(BF16)
    dst[row, :, chans : 2 * chans] = values.astype(BF16)
    dst[row, :, 2 * chans : 3 * chans] = after.astype(BF16)


def product(source, weights, row):
    lhs = jnp.concatenate([source[row + i] for i in range(3)], axis=-1)
    return jnp.dot(lhs, weights[...], preferred_element_type=F32)


def send(base, change, frame, index, held, out, sems):
    mixed = (base.astype(F32) + change).astype(BF16)
    held[frame, index] = mixed.reshape(held.shape[2:])
    copy = pltpu.make_async_copy(
        held.at[frame, index], out.at[:, frame, index], sems.at[frame, index]
    )
    copy.start()
    return copy


def inner_body(info, inner, outer, halo, gain_one, w_one, gain_two, w_two,
               out, shared, s_one, s_two, kept, held, kept_sems, sems):
    frames, _, width, chans = inner.shape
    odd = info[0] == 1
    half_one = gain_one[...] * 0.5
    half_two = gain_two[...] * 0.5

    def put_first(frame, index):
        if index < HALF:
            raw = jnp.where(odd, halo[frame, index], outer[frame, index])
        elif index < 2 * HALF:
            raw = inner[frame, index - HALF]
        else:
            raw = jnp.where(odd, outer[frame, index - 2 * HALF], halo[frame, index - 2 * HALF])
        put_shifted(s_one.at[frame], index, silu_from_half(scaled(raw.astype(F32), half_one)))

    def put_second(frame, index):
        hidden = product(s_one.at[frame], w_one, index)
        put_shifted(s_two.at[frame], index, silu_from_half(scaled(hidden, half_two)))

    for index in range(3 * HALF):
        put_first(0, index)
    copies = []
    for frame in range(frames):
        for index in range(2 * HALF):
            if frame + 1 < frames:
                for ahead in range(index * 3 // 2, (index + 1) * 3 // 2):
                    put_first(frame + 1, ahead)
            put_second(frame, index)
    for frame in range(frames):
        here = slice(chans, 2 * chans)
        for index in range(HALF):
            kept[frame, index] = jnp.where(
                odd, s_two[frame, HALF + index, :, here], s_two[frame, index, :, here]
            )
        copy = pltpu.make_async_copy(kept.at[frame], shared.at[frame], kept_sems.at[frame])
        copy.start()
        copies.append(copy)
        for index in range(HALF):
            change = product(s_two.at[frame], w_two, index)
            copies.append(send(inner[frame, index], change, frame, index, held, out, sems))
    for copy in copies:
        copy.wait()


def outer_body(info, outer, halo, shared, gain_one, w_one, gain_two, conv_two,
               out, s_one, s_two_a, s_two_b, kept, w_two, held, kept_sems, w_sem, sems):
    frames, _, width, chans = outer.shape
    odd, goes_on = info[0] == 1, info[1] == 1
    new_at = jnp.where(odd, HALF, 0)
    shared_at = HALF - new_at
    half_one = gain_one[...] * 0.5
    half_two = gain_two[...] * 0.5
    s_two = (s_two_a, s_two_b)
    fetch = pltpu.make_async_copy(shared, kept, kept_sems.at[0])
    load = pltpu.make_async_copy(conv_two, w_two, w_sem)
    fetch.start()
    load.start()

    def put_first(frame, index):
        if index < HALF:
            raw = jnp.where(odd, outer[frame, index], halo[frame, index])
        else:
            raw = jnp.where(odd, halo[frame, index - HALF], outer[frame, index - HALF])
        put_shifted(s_one.at[frame], index, silu_from_half(scaled(raw.astype(F32), half_one)))

    def put_second(frame, index):
        hidden = product(s_one.at[frame], w_one, index)
        second = silu_from_half(scaled(hidden, half_two))
        outside = jnp.logical_not(goes_on) & (odd if index == HALF - 1 else jnp.logical_not(odd))
        second = jnp.where(outside, 0.0, second)
        put_shifted(s_two[frame], new_at + index, second)

    for index in range(2 * HALF):
        put_first(0, index)
    for frame in range(frames):
        for index in range(HALF):
            if frame + 1 < frames:
                for ahead in range(2 * index, 2 * index + 2):
                    put_first(frame + 1, ahead)
            put_second(frame, index)
        if frame == 0:
            fetch.wait()
            load.wait()
        for index in range(HALF):
            put_shifted(s_two[frame], shared_at + index, kept[frame, index].astype(F32))
    copies = []
    for frame in range(frames):
        for index in range(HALF):
            change = product(s_two[frame], w_two, index)
            copies.append(send(outer[frame, index], change, frame, index, held, out, sems))
    for copy in copies:
        copy.wait()


def conv_chunk(info, inner, outer, halo, shared, owners, weights):
    frames, _, cols, chans = outer.shape
    own = cols // owners
    is_outer = shared is not None
    stack = lambda count: pltpu.VMEM((frames, count, cols, 3 * chans), BF16)
    here = pl.BlockSpec(memory_space=pltpu.VMEM)
    there = pl.BlockSpec(memory_space=pltpu.HBM)
    near = lambda v: pltpu.with_memory_space_constraint(v, pltpu.VMEM)
    far = lambda v: pltpu.with_memory_space_constraint(v, pltpu.HBM)
    gain_one, conv_one, gain_two, conv_two = weights
    mixed = pltpu.HBM((owners, frames, HALF, own, chans), BF16)
    keep = pltpu.HBM((frames, HALF, cols, chans), BF16)
    first_rows = (2 if is_outer else 3) * HALF
    new_rows = (1 if is_outer else 2) * HALF
    flops = 2 * frames * (new_rows + HALF) * cols * 9 * chans * chans
    two = [pltpu.VMEM((2 * HALF, cols, 3 * chans), BF16)] * 2 if is_outer else [stack(2 * HALF)]
    return pl.pallas_call(
        outer_body if is_outer else inner_body,
        in_specs=[
            pl.BlockSpec(memory_space=pltpu.SMEM), here, here, there if is_outer else here,
            here, here, here, there if is_outer else here,
        ],
        out_specs=[there] if is_outer else [there, there],
        out_shape=[mixed] if is_outer else [mixed, keep],
        scratch_shapes=[
            stack(first_rows),
            *two,
            pltpu.VMEM((frames, HALF, cols, chans), BF16),
            *([pltpu.VMEM(conv_two.shape, BF16)] if is_outer else []),
            pltpu.VMEM((frames, HALF, owners, own, chans), BF16),
            pltpu.SemaphoreType.DMA((frames,)),
            *([pltpu.SemaphoreType.DMA] if is_outer else []),
            pltpu.SemaphoreType.DMA((frames, HALF)),
        ],
        compiler_params=pltpu.CompilerParams(vmem_limit_bytes=28 * 1024 * 1024),
        cost_estimate=pl.CostEstimate(
            flops=flops, bytes_accessed=8 * 1024 * 1024, transcendentals=0
        ),
        name="convs_outer" if is_outer else "convs_inner",
    )(
        info, *((outer, halo, far(shared)) if is_outer else (inner, outer, halo)),
        gain_one, near(conv_one), gain_two, far(conv_two) if is_outer else near(conv_two),
    )


def attend_body(group, order, x_ref, gain_three, kernel, gain_four, wq, wk, wv, wo, *refs):
    frames, pixels, chans = x_ref.shape
    count = frames * pixels
    half_three = gain_three[...] * 0.5
    x = x_ref[...].reshape(count, chans).astype(F32)
    third = silu_from_half(scaled(x, half_three)).astype(BF16).reshape(frames, pixels, chans)
    one = jnp.concatenate([third[:1], third[:-1]], axis=0)
    two = jnp.concatenate([third[:1], third[:1], third[:-2]], axis=0)
    taps = jnp.concatenate([two, one, third], axis=-1).reshape(count, 3 * chans)
    timed = x + jnp.dot(taps, kernel[...], preferred_element_type=F32)
    fourth = scaled(timed, gain_four[...]).astype(BF16)
    project = lambda w: jnp.dot(fourth, w[...], preferred_element_type=F32)
    scale = 1.0 / float(chans) ** 0.5
    queries = (project(wq) * scale).astype(BF16).reshape(frames, pixels, chans)
    keys = project(wk).astype(BF16).reshape(frames, pixels, chans)
    values = project(wv).astype(BF16).reshape(frames, pixels, chans)
    size = frames * group
    down = lax.broadcasted_iota(jnp.int32, (size, size), 0)
    along = lax.broadcasted_iota(jnp.int32, (size, size), 1)
    allowed = (down % group == along % group) & (down >= along)
    pieces = []
    for g in range(pixels // group):
        cut = lambda v: v[:, g * group : (g + 1) * group].reshape(size, chans)
        scores = lax.dot_general(
            cut(queries), cut(keys), (((1,), (1,)), ((), ())), preferred_element_type=F32
        )
        scores = jnp.where(allowed, scores, -1e30)
        top = jnp.max(scores, axis=-1, keepdims=True)
        weights = jnp.exp(scores - top)
        total = jnp.sum(weights, axis=-1, keepdims=True)
        weights = (weights * (1.0 / total)).astype(BF16)
        attended = jnp.dot(weights, cut(values), preferred_element_type=F32)
        pieces.append(attended.astype(BF16).reshape(frames, group, chans))
    attended = pieces[0] if len(pieces) == 1 else jnp.concatenate(pieces, axis=1)
    final = timed + jnp.dot(
        attended.reshape(count, chans), wo[...], preferred_element_type=F32
    )
    final = final.astype(BF16).reshape(frames, pixels, chans)
    if len(refs) == 1:
        refs[0][...] = final
        return
    *outs, held = refs
    held[...] = final
    share = frames // len(outs)
    for n, out in enumerate(outs):
        out[...] = held[pl.ds(order[n] * share, share)]


def attend_chunk(x, order, weights, tile, group, members=0):
    frames, pixels, chans = x.shape
    tile = min(tile, pixels)
    near = lambda v: pltpu.with_memory_space_constraint(v, pltpu.VMEM)
    whole = lambda a: pl.BlockSpec(a.shape, lambda p: (0,) * a.ndim)
    count, share = (members, frames // members) if members else (1, frames)
    block = lambda depth: pl.BlockSpec((depth, tile, chans), lambda p: (0, p, 0))
    result = pl.pallas_call(
        functools.partial(attend_body, group),
        grid=(pixels // tile,),
        in_specs=[pl.BlockSpec(memory_space=pltpu.SMEM), block(frames)]
        + [whole(w) for w in weights],
        out_specs=[block(share)] * count,
        out_shape=[pltpu.HBM((share, pixels, chans), BF16)] * count,
        scratch_shapes=[pltpu.VMEM((frames, tile, chans), BF16)] if members else [],
        compiler_params=pltpu.CompilerParams(vmem_limit_bytes=32 * 1024 * 1024),
        cost_estimate=pl.CostEstimate(
            flops=2 * frames * pixels * chans * chans * 9,
            bytes_accessed=4 * 1024 * 1024,
            transcendentals=0,
        ),
        name="attend",
    )(order, x, *[w if w.shape[0] == 1 else near(w) for w in weights])
    return result if members else result[0]


def place_body(count, where, *refs):
    pieces, (out, sems) = refs[:count], refs[-2:]
    if count == 1:
        pieces = [(n, pieces[0].at[n]) for n in range(pieces[0].shape[0])]
    else:
        pieces = [(where[1 + n], piece) for n, piece in enumerate(pieces)]
    rows, own = pieces[0][1].shape[1:3]
    copies = []
    for n, (member, piece) in enumerate(pieces):
        columns = pl.ds(pl.multiple_of(member * own, own), own)
        copies.append(
            pltpu.make_async_copy(piece, out.at[:, pl.ds(where[0], rows), columns], sems.at[n])
        )
    for copy in copies:
        copy.start()
    for copy in copies:
        copy.wait()


def place(where, pieces, shape, result=None):
    here = pl.BlockSpec(memory_space=pltpu.VMEM)
    there = pl.BlockSpec(memory_space=pltpu.HBM)
    scalars = pl.BlockSpec(memory_space=pltpu.SMEM)
    given = [] if result is None else [result]
    return pl.pallas_call(
        functools.partial(place_body, len(pieces)),
        in_specs=[scalars] + [here] * len(pieces) + [there] * len(given),
        out_specs=there,
        out_shape=pltpu.HBM(shape, BF16),
        input_output_aliases={1 + len(pieces): 0} if given else {},
        scratch_shapes=[pltpu.SemaphoreType.DMA((where.shape[0],))],
        compiler_params=pltpu.CompilerParams(vmem_limit_bytes=16 * 1024 * 1024),
        cost_estimate=pl.CostEstimate(
            flops=0, bytes_accessed=2 * 1024 * 1024, transcendentals=0
        ),
        name="place",
    )(where, *[pltpu.with_memory_space_constraint(v, pltpu.VMEM) for v in pieces], *given)


def cut_body(start, video, part, sem):
    copy = pltpu.make_async_copy(video.at[:, pl.ds(start[0], HALF)], part, sem)
    copy.start()
    copy.wait()


def cut(start, video):
    frames, rows, cols, chans = video.shape
    return pl.pallas_call(
        cut_body,
        in_specs=[
            pl.BlockSpec(memory_space=pltpu.SMEM), pl.BlockSpec(memory_space=pltpu.HBM),
        ],
        out_specs=pl.BlockSpec(memory_space=pltpu.VMEM),
        out_shape=pltpu.VMEM((frames, HALF, cols, chans), BF16),
        scratch_shapes=[pltpu.SemaphoreType.DMA],
        compiler_params=pltpu.CompilerParams(vmem_limit_bytes=8 * 1024 * 1024),
        cost_estimate=pl.CostEstimate(
            flops=0, bytes_accessed=2 * 1024 * 1024, transcendentals=0
        ),
        name="cut",
    )(start, pltpu.with_memory_space_constraint(video, pltpu.HBM))


def shards(
    video,
    gain_one,
    conv_one,
    gain_two,
    conv_two,
    gain_three,
    time_kernel,
    gain_four,
    query_weight,
    key_weight,
    value_weight,
    out_weight,
):
    owners = lax.axis_size("tm")
    strips = lax.axis_size("strip")
    strip = lax.axis_index("strip")
    chans = video.shape[-1]
    odd = strip % 2
    siblings = [(i, i ^ 1) for i in range(strips)]
    neighbours = [(i, i + 1 if i % 2 else i - 1) for i in range(1, strips - 1)]
    inner_start = HALF - HALF * odd
    outer_start = HALF * odd
    goes_on = (strip > 0) & (strip < strips - 1)
    info = jnp.stack([odd, goes_on.astype(jnp.int32)])
    row = lambda gain: gain.reshape(1, chans)
    flat = lambda w: w.reshape(-1, chans)
    conv_weights = (row(gain_one), flat(conv_one), row(gain_two), flat(conv_two))
    attend_weights = (
        row(gain_three), flat(time_kernel), row(gain_four),
        query_weight, key_weight, value_weight, out_weight,
    )
    starts = jnp.stack([inner_start, outer_start])
    outer = cut(starts[1:], video)
    from_outer = lax.ppermute(outer, "strip", neighbours)
    inner = cut(starts[:1], video)
    from_sibling = lax.ppermute(inner, "strip", siblings)

    me = lax.axis_index("tm")
    sides = owners // 2
    steps = [(0, 0), (0, 1), (1, 0), (1, 1), (3, 0), (3, 1), (2, 1), (2, 0)]
    member = lambda i, dy, dx: (i // 2 + dy) % sides * 2 + (i + dx) % 2
    to = jnp.stack([member(me, dy, dx) for dy, dx in steps])
    source = jnp.stack([member(me, sides - dy, dx) for dy, dx in steps])
    exchange = lambda v: lax.all_to_all(v, "tm", split_axis=0, concat_axis=0, tiled=True)

    mixed, shared = conv_chunk(info, inner, outer, from_sibling, None, owners, conv_weights)
    block = exchange(mixed)
    by_frame = (owners * block.shape[1], -1, chans)
    final = attend_chunk(block.reshape(by_frame), to, attend_weights, 128, 16)
    (mixed,) = conv_chunk(info, inner, outer, from_outer, shared, owners, conv_weights)
    block = exchange(mixed)
    finals = attend_chunk(block.reshape(by_frame), to, attend_weights, 128, 16, owners)
    back = exchange(final.reshape(block.shape))
    where = jnp.concatenate([starts[1:], source])
    result = place(jnp.broadcast_to(starts[:1], where.shape), [back], video.shape)
    backs = [finals[0]] + [
        lax.ppermute(finals[n], "tm", [(i, member(i, dy, dx)) for i in range(owners)])
        for n, (dy, dx) in enumerate(steps)
        if n
    ]
    backs = [v.reshape(block.shape[1:]) for v in backs]
    return place(where, backs, video.shape, result)


def solution(mesh):
    placed = (P("tm", "strip", None, None), P(), P(), P(), P(), P(), P(), P(), P(), P(), P(), P())
    return jax.shard_map(
        shards, mesh=mesh, in_specs=placed, out_specs=P("tm", "strip", None, None), check_vma=False
    )
```

```python
import functools

import jax
import jax.numpy as jnp
from jax import lax
from jax.experimental import pallas as pl
from jax.experimental.pallas import tpu as pltpu
from jax.sharding import PartitionSpec as P

BF16 = jnp.bfloat16
F32 = jnp.float32
EPS = 1e-06
HALF = 2


def scaled(values, gain):
    mean = jnp.mean(values * values, axis=-1, keepdims=True)
    return values * lax.rsqrt(mean + EPS) * gain


def silu_from_half(half):
    return half + half * jnp.tanh(half)


def put_shifted(dst, row, values):
    width, chans = values.shape
    index = lax.broadcasted_iota(jnp.int32, (width, 1), 0)
    before = jnp.where(index == 0, 0.0, pltpu.roll(values, 1, 0))
    after = jnp.where(index == width - 1, 0.0, pltpu.roll(values, width - 1, 0))
    dst[row, :, 0:chans] = before.astype(BF16)
    dst[row, :, chans : 2 * chans] = values.astype(BF16)
    dst[row, :, 2 * chans : 3 * chans] = after.astype(BF16)


def product(source, weights, row):
    lhs = jnp.concatenate([source[row + i] for i in range(3)], axis=-1)
    return jnp.dot(lhs, weights[...], preferred_element_type=F32)


def send(base, change, frame, index, held, out, sems):
    mixed = (base.astype(F32) + change).astype(BF16)
    held[frame, index] = mixed.reshape(held.shape[2:])
    copy = pltpu.make_async_copy(
        held.at[frame, index], out.at[:, frame, index], sems.at[frame, index]
    )
    copy.start()
    return copy


def inner_body(info, inner, outer, halo, gain_one, w_one, gain_two, w_two,
               out, shared, s_one, s_two, kept, held, kept_sems, sems):
    frames, _, width, chans = inner.shape
    odd = info[0] == 1
    half_one = gain_one[...] * 0.5
    half_two = gain_two[...] * 0.5

    def put_first(frame, index):
        if index < HALF:
            raw = jnp.where(odd, halo[frame, index], outer[frame, index])
        elif index < 2 * HALF:
            raw = inner[frame, index - HALF]
        else:
            raw = jnp.where(odd, outer[frame, index - 2 * HALF], halo[frame, index - 2 * HALF])
        put_shifted(s_one.at[frame], index, silu_from_half(scaled(raw.astype(F32), half_one)))

    def put_second(frame, index):
        hidden = product(s_one.at[frame], w_one, index)
        put_shifted(s_two.at[frame], index, silu_from_half(scaled(hidden, half_two)))

    for index in range(3 * HALF):
        put_first(0, index)
    copies = []
    for frame in range(frames):
        for index in range(2 * HALF):
            if frame + 1 < frames:
                for ahead in range(index * 3 // 2, (index + 1) * 3 // 2):
                    put_first(frame + 1, ahead)
            put_second(frame, index)
    for frame in range(frames):
        here = slice(chans, 2 * chans)
        for index in range(HALF):
            kept[frame, index] = jnp.where(
                odd, s_two[frame, HALF + index, :, here], s_two[frame, index, :, here]
            )
        copy = pltpu.make_async_copy(kept.at[frame], shared.at[frame], kept_sems.at[frame])
        copy.start()
        copies.append(copy)
        for index in range(HALF):
            change = product(s_two.at[frame], w_two, index)
            copies.append(send(inner[frame, index], change, frame, index, held, out, sems))
    for copy in copies:
        copy.wait()


def outer_body(info, outer, halo, shared, gain_one, w_one, gain_two, conv_two,
               out, s_one, s_two_a, s_two_b, kept, w_two, held, kept_sems, w_sem, sems):
    frames, _, width, chans = outer.shape
    odd, goes_on = info[0] == 1, info[1] == 1
    new_at = jnp.where(odd, HALF, 0)
    shared_at = HALF - new_at
    half_one = gain_one[...] * 0.5
    half_two = gain_two[...] * 0.5
    s_two = (s_two_a, s_two_b)
    fetch = pltpu.make_async_copy(shared, kept, kept_sems.at[0])
    load = pltpu.make_async_copy(conv_two, w_two, w_sem)
    fetch.start()
    load.start()

    def put_first(frame, index):
        if index < HALF:
            raw = jnp.where(odd, outer[frame, index], halo[frame, index])
        else:
            raw = jnp.where(odd, halo[frame, index - HALF], outer[frame, index - HALF])
        put_shifted(s_one.at[frame], index, silu_from_half(scaled(raw.astype(F32), half_one)))

    def put_second(frame, index):
        hidden = product(s_one.at[frame], w_one, index)
        second = silu_from_half(scaled(hidden, half_two))
        outside = jnp.logical_not(goes_on) & (odd if index == HALF - 1 else jnp.logical_not(odd))
        second = jnp.where(outside, 0.0, second)
        put_shifted(s_two[frame], new_at + index, second)

    for index in range(2 * HALF):
        put_first(0, index)
    for frame in range(frames):
        for index in range(HALF):
            if frame + 1 < frames:
                for ahead in range(2 * index, 2 * index + 2):
                    put_first(frame + 1, ahead)
            put_second(frame, index)
        if frame == 0:
            fetch.wait()
            load.wait()
        for index in range(HALF):
            put_shifted(s_two[frame], shared_at + index, kept[frame, index].astype(F32))
    copies = []
    for frame in range(frames):
        for index in range(HALF):
            change = product(s_two[frame], w_two, index)
            copies.append(send(outer[frame, index], change, frame, index, held, out, sems))
    for copy in copies:
        copy.wait()


def conv_chunk(info, inner, outer, halo, shared, owners, weights):
    frames, _, cols, chans = outer.shape
    own = cols // owners
    is_outer = shared is not None
    stack = lambda count: pltpu.VMEM((frames, count, cols, 3 * chans), BF16)
    here = pl.BlockSpec(memory_space=pltpu.VMEM)
    there = pl.BlockSpec(memory_space=pltpu.HBM)
    near = lambda v: pltpu.with_memory_space_constraint(v, pltpu.VMEM)
    far = lambda v: pltpu.with_memory_space_constraint(v, pltpu.HBM)
    gain_one, conv_one, gain_two, conv_two = weights
    mixed = pltpu.HBM((owners, frames, HALF, own, chans), BF16)
    keep = pltpu.HBM((frames, HALF, cols, chans), BF16)
    first_rows = (2 if is_outer else 3) * HALF
    new_rows = (1 if is_outer else 2) * HALF
    flops = 2 * frames * (new_rows + HALF) * cols * 9 * chans * chans
    two = [pltpu.VMEM((2 * HALF, cols, 3 * chans), BF16)] * 2 if is_outer else [stack(2 * HALF)]
    return pl.pallas_call(
        outer_body if is_outer else inner_body,
        in_specs=[
            pl.BlockSpec(memory_space=pltpu.SMEM), here, here, there if is_outer else here,
            here, here, here, there if is_outer else here,
        ],
        out_specs=[there] if is_outer else [there, there],
        out_shape=[mixed] if is_outer else [mixed, keep],
        scratch_shapes=[
            stack(first_rows),
            *two,
            pltpu.VMEM((frames, HALF, cols, chans), BF16),
            *([pltpu.VMEM(conv_two.shape, BF16)] if is_outer else []),
            pltpu.VMEM((frames, HALF, owners, own, chans), BF16),
            pltpu.SemaphoreType.DMA((frames,)),
            *([pltpu.SemaphoreType.DMA] if is_outer else []),
            pltpu.SemaphoreType.DMA((frames, HALF)),
        ],
        compiler_params=pltpu.CompilerParams(vmem_limit_bytes=28 * 1024 * 1024),
        cost_estimate=pl.CostEstimate(
            flops=flops, bytes_accessed=8 * 1024 * 1024, transcendentals=0
        ),
        name="convs_outer" if is_outer else "convs_inner",
    )(
        info, *((outer, halo, far(shared)) if is_outer else (inner, outer, halo)),
        gain_one, near(conv_one), gain_two, far(conv_two) if is_outer else near(conv_two),
    )


def attend_body(group, order, x_ref, gain_three, kernel, gain_four, wq, wk, wv, wo, *refs):
    frames, pixels, chans = x_ref.shape
    count = frames * pixels
    half_three = gain_three[...] * 0.5
    x = x_ref[...].reshape(count, chans).astype(F32)
    third = silu_from_half(scaled(x, half_three)).astype(BF16).reshape(frames, pixels, chans)
    one = jnp.concatenate([third[:1], third[:-1]], axis=0)
    two = jnp.concatenate([third[:1], third[:1], third[:-2]], axis=0)
    taps = jnp.concatenate([two, one, third], axis=-1).reshape(count, 3 * chans)
    timed = x + jnp.dot(taps, kernel[...], preferred_element_type=F32)
    fourth = scaled(timed, gain_four[...]).astype(BF16)
    project = lambda w: jnp.dot(fourth, w[...], preferred_element_type=F32)
    scale = 1.0 / float(chans) ** 0.5
    queries = (project(wq) * scale).astype(BF16).reshape(frames, pixels, chans)
    keys = project(wk).astype(BF16).reshape(frames, pixels, chans)
    values = project(wv).astype(BF16).reshape(frames, pixels, chans)
    size = frames * group
    down = lax.broadcasted_iota(jnp.int32, (size, size), 0)
    along = lax.broadcasted_iota(jnp.int32, (size, size), 1)
    allowed = (down % group == along % group) & (down >= along)
    pieces = []
    for g in range(pixels // group):
        cut = lambda v: v[:, g * group : (g + 1) * group].reshape(size, chans)
        scores = lax.dot_general(
            cut(queries), cut(keys), (((1,), (1,)), ((), ())), preferred_element_type=F32
        )
        scores = jnp.where(allowed, scores, -1e30)
        top = jnp.max(scores, axis=-1, keepdims=True)
        weights = jnp.exp(scores - top)
        total = jnp.sum(weights, axis=-1, keepdims=True)
        weights = (weights * (1.0 / total)).astype(BF16)
        attended = jnp.dot(weights, cut(values), preferred_element_type=F32)
        pieces.append(attended.astype(BF16).reshape(frames, group, chans))
    attended = pieces[0] if len(pieces) == 1 else jnp.concatenate(pieces, axis=1)
    final = timed + jnp.dot(
        attended.reshape(count, chans), wo[...], preferred_element_type=F32
    )
    final = final.astype(BF16).reshape(frames, pixels, chans)
    if len(refs) == 1:
        refs[0][...] = final
        return
    *outs, held = refs
    held[...] = final
    share = frames // len(outs)
    for n, out in enumerate(outs):
        out[...] = held[pl.ds(order[n] * share, share)]


def attend_chunk(x, order, weights, tile, group, members=0):
    frames, pixels, chans = x.shape
    tile = min(tile, pixels)
    near = lambda v: pltpu.with_memory_space_constraint(v, pltpu.VMEM)
    whole = lambda a: pl.BlockSpec(a.shape, lambda p: (0,) * a.ndim)
    count, share = (members, frames // members) if members else (1, frames)
    block = lambda depth: pl.BlockSpec((depth, tile, chans), lambda p: (0, p, 0))
    result = pl.pallas_call(
        functools.partial(attend_body, group),
        grid=(pixels // tile,),
        in_specs=[pl.BlockSpec(memory_space=pltpu.SMEM), block(frames)]
        + [whole(w) for w in weights],
        out_specs=[block(share)] * count,
        out_shape=[pltpu.HBM((share, pixels, chans), BF16)] * count,
        scratch_shapes=[pltpu.VMEM((frames, tile, chans), BF16)] if members else [],
        compiler_params=pltpu.CompilerParams(vmem_limit_bytes=32 * 1024 * 1024),
        cost_estimate=pl.CostEstimate(
            flops=2 * frames * pixels * chans * chans * 9,
            bytes_accessed=4 * 1024 * 1024,
            transcendentals=0,
        ),
        name="attend",
    )(order, x, *[w if w.shape[0] == 1 else near(w) for w in weights])
    return result if members else result[0]


def place_body(count, where, *refs):
    pieces, (out, sems) = refs[:count], refs[-2:]
    if count == 1:
        pieces = [(n, pieces[0].at[n]) for n in range(pieces[0].shape[0])]
    else:
        pieces = [(where[1 + n], piece) for n, piece in enumerate(pieces)]
    rows, own = pieces[0][1].shape[1:3]
    copies = []
    for n, (member, piece) in enumerate(pieces):
        columns = pl.ds(pl.multiple_of(member * own, own), own)
        copies.append(
            pltpu.make_async_copy(piece, out.at[:, pl.ds(where[0], rows), columns], sems.at[n])
        )
    for copy in copies:
        copy.start()
    for copy in copies:
        copy.wait()


def place(where, pieces, shape, result=None):
    here = pl.BlockSpec(memory_space=pltpu.VMEM)
    there = pl.BlockSpec(memory_space=pltpu.HBM)
    scalars = pl.BlockSpec(memory_space=pltpu.SMEM)
    given = [] if result is None else [result]
    return pl.pallas_call(
        functools.partial(place_body, len(pieces)),
        in_specs=[scalars] + [here] * len(pieces) + [there] * len(given),
        out_specs=there,
        out_shape=pltpu.HBM(shape, BF16),
        input_output_aliases={1 + len(pieces): 0} if given else {},
        scratch_shapes=[pltpu.SemaphoreType.DMA((where.shape[0],))],
        compiler_params=pltpu.CompilerParams(vmem_limit_bytes=16 * 1024 * 1024),
        cost_estimate=pl.CostEstimate(
            flops=0, bytes_accessed=2 * 1024 * 1024, transcendentals=0
        ),
        name="place",
    )(where, *[pltpu.with_memory_space_constraint(v, pltpu.VMEM) for v in pieces], *given)


def cut_body(start, video, part, sem):
    copy = pltpu.make_async_copy(video.at[:, pl.ds(start[0], HALF)], part, sem)
    copy.start()
    copy.wait()


def cut(start, video):
    frames, rows, cols, chans = video.shape
    return pl.pallas_call(
        cut_body,
        in_specs=[
            pl.BlockSpec(memory_space=pltpu.SMEM), pl.BlockSpec(memory_space=pltpu.HBM),
        ],
        out_specs=pl.BlockSpec(memory_space=pltpu.VMEM),
        out_shape=pltpu.VMEM((frames, HALF, cols, chans), BF16),
        scratch_shapes=[pltpu.SemaphoreType.DMA],
        compiler_params=pltpu.CompilerParams(vmem_limit_bytes=8 * 1024 * 1024),
        cost_estimate=pl.CostEstimate(
            flops=0, bytes_accessed=2 * 1024 * 1024, transcendentals=0
        ),
        name="cut",
    )(start, pltpu.with_memory_space_constraint(video, pltpu.HBM))


def shards(
    video,
    gain_one,
    conv_one,
    gain_two,
    conv_two,
    gain_three,
    time_kernel,
    gain_four,
    query_weight,
    key_weight,
    value_weight,
    out_weight,
):
    owners = lax.axis_size("tm")
    strips = lax.axis_size("strip")
    strip = lax.axis_index("strip")
    chans = video.shape[-1]
    odd = strip % 2
    siblings = [(i, i ^ 1) for i in range(strips)]
    neighbours = [(i, i + 1 if i % 2 else i - 1) for i in range(1, strips - 1)]
    inner_start = HALF - HALF * odd
    outer_start = HALF * odd
    goes_on = (strip > 0) & (strip < strips - 1)
    info = jnp.stack([odd, goes_on.astype(jnp.int32)])
    row = lambda gain: gain.reshape(1, chans)
    flat = lambda w: w.reshape(-1, chans)
    conv_weights = (row(gain_one), flat(conv_one), row(gain_two), flat(conv_two))
    attend_weights = (
        row(gain_three), flat(time_kernel), row(gain_four),
        query_weight, key_weight, value_weight, out_weight,
    )
    starts = jnp.stack([inner_start, outer_start])
    outer = cut(starts[1:], video)
    from_outer = lax.ppermute(outer, "strip", neighbours)
    inner = cut(starts[:1], video)
    from_sibling = lax.ppermute(inner, "strip", siblings)

    me = lax.axis_index("tm")
    sides = owners // 2
    steps = [(0, 0), (2, 1), (1, 1), (3, 1), (2, 0), (0, 1), (1, 0), (3, 0)]
    member = lambda i, dy, dx: (i // 2 + dy) % sides * 2 + (i + dx) % 2
    to = jnp.stack([member(me, dy, dx) for dy, dx in steps])
    source = jnp.stack([member(me, sides - dy, dx) for dy, dx in steps])
    exchange = lambda v: lax.all_to_all(v, "tm", split_axis=0, concat_axis=0, tiled=True)

    mixed, shared = conv_chunk(info, inner, outer, from_sibling, None, owners, conv_weights)
    block = exchange(mixed)
    by_frame = (owners * block.shape[1], -1, chans)
    final = attend_chunk(block.reshape(by_frame), to, attend_weights, 128, 16)
    (mixed,) = conv_chunk(info, inner, outer, from_outer, shared, owners, conv_weights)
    block = exchange(mixed)
    finals = attend_chunk(block.reshape(by_frame), to, attend_weights, 128, 16, owners)
    back = exchange(final.reshape(block.shape))
    where = jnp.concatenate([starts[1:], source])
    result = place(jnp.broadcast_to(starts[:1], where.shape), [back], video.shape)
    backs = [finals[0]] + [
        lax.ppermute(finals[n], "tm", [(i, member(i, dy, dx)) for i in range(owners)])
        for n, (dy, dx) in enumerate(steps)
        if n
    ]
    backs = [v.reshape(block.shape[1:]) for v in backs]
    return place(where, backs, video.shape, result)


def solution(mesh):
    placed = (P("tm", "strip", None, None), P(), P(), P(), P(), P(), P(), P(), P(), P(), P(), P())
    return jax.shard_map(
        shards, mesh=mesh, in_specs=placed, out_specs=P("tm", "strip", None, None), check_vma=False
    )
```

```python
import functools

import jax
import jax.numpy as jnp
from jax import lax
from jax.experimental import pallas as pl
from jax.experimental.pallas import tpu as pltpu
from jax.sharding import PartitionSpec as P

BF16 = jnp.bfloat16
F32 = jnp.float32
EPS = 1e-06
HALF = 2


def scaled(values, gain):
    mean = jnp.mean(values * values, axis=-1, keepdims=True)
    return values * lax.rsqrt(mean + EPS) * gain


def silu_from_half(half):
    return half + half * jnp.tanh(half)


def put_shifted(dst, row, values):
    width, chans = values.shape
    index = lax.broadcasted_iota(jnp.int32, (width, 1), 0)
    before = jnp.where(index == 0, 0.0, pltpu.roll(values, 1, 0))
    after = jnp.where(index == width - 1, 0.0, pltpu.roll(values, width - 1, 0))
    dst[row, :, 0:chans] = before.astype(BF16)
    dst[row, :, chans : 2 * chans] = values.astype(BF16)
    dst[row, :, 2 * chans : 3 * chans] = after.astype(BF16)


def product(source, weights, row):
    lhs = jnp.concatenate([source[row + i] for i in range(3)], axis=-1)
    return jnp.dot(lhs, weights[...], preferred_element_type=F32)


def send(base, change, frame, index, held, out, sems):
    mixed = (base.astype(F32) + change).astype(BF16)
    held[frame, index] = mixed.reshape(held.shape[2:])
    copy = pltpu.make_async_copy(
        held.at[frame, index], out.at[:, frame, index], sems.at[frame, index]
    )
    copy.start()
    return copy


def inner_body(info, inner, outer, halo, gain_one, w_one, gain_two, conv_two,
               out, shared, s_one, s_two, kept, w_two, held, kept_sems, w_sem, sems):
    frames, _, width, chans = inner.shape
    odd = info[0] == 1
    half_one = gain_one[...] * 0.5
    half_two = gain_two[...] * 0.5
    load = pltpu.make_async_copy(conv_two, w_two, w_sem)
    load.start()

    def put_first(frame, index):
        if index < HALF:
            raw = jnp.where(odd, halo[frame, index], outer[frame, index])
        elif index < 2 * HALF:
            raw = inner[frame, index - HALF]
        else:
            raw = jnp.where(odd, outer[frame, index - 2 * HALF], halo[frame, index - 2 * HALF])
        put_shifted(s_one.at[frame], index, silu_from_half(scaled(raw.astype(F32), half_one)))

    def put_second(frame, index):
        hidden = product(s_one.at[frame], w_one, index)
        put_shifted(s_two.at[frame], index, silu_from_half(scaled(hidden, half_two)))

    for index in range(3 * HALF):
        put_first(0, index)
    load.wait()
    copies = []
    for frame in range(frames):
        for index in range(2 * HALF):
            if frame + 1 < frames:
                for ahead in range(index * 3 // 2, (index + 1) * 3 // 2):
                    put_first(frame + 1, ahead)
            put_second(frame, index)
    for frame in range(frames):
        here = slice(chans, 2 * chans)
        for index in range(HALF):
            kept[frame, index] = jnp.where(
                odd, s_two[frame, HALF + index, :, here], s_two[frame, index, :, here]
            )
        copy = pltpu.make_async_copy(kept.at[frame], shared.at[frame], kept_sems.at[frame])
        copy.start()
        copies.append(copy)
        for index in range(HALF):
            change = product(s_two.at[frame], w_two, index)
            copies.append(send(inner[frame, index], change, frame, index, held, out, sems))
    for copy in copies:
        copy.wait()


def outer_body(info, outer, halo, shared, gain_one, w_one, gain_two, conv_two,
               out, s_one, s_two_a, s_two_b, kept, w_two, held, kept_sems, w_sem, sems):
    frames, _, width, chans = outer.shape
    odd, goes_on = info[0] == 1, info[1] == 1
    new_at = jnp.where(odd, HALF, 0)
    shared_at = HALF - new_at
    half_one = gain_one[...] * 0.5
    half_two = gain_two[...] * 0.5
    s_two = (s_two_a, s_two_b)
    fetch = pltpu.make_async_copy(shared, kept, kept_sems.at[0])
    load = pltpu.make_async_copy(conv_two, w_two, w_sem)
    fetch.start()
    load.start()

    def put_first(frame, index):
        if index < HALF:
            raw = jnp.where(odd, outer[frame, index], halo[frame, index])
        else:
            raw = jnp.where(odd, halo[frame, index - HALF], outer[frame, index - HALF])
        put_shifted(s_one.at[frame], index, silu_from_half(scaled(raw.astype(F32), half_one)))

    def put_second(frame, index):
        hidden = product(s_one.at[frame], w_one, index)
        second = silu_from_half(scaled(hidden, half_two))
        outside = jnp.logical_not(goes_on) & (odd if index == HALF - 1 else jnp.logical_not(odd))
        second = jnp.where(outside, 0.0, second)
        put_shifted(s_two[frame], new_at + index, second)

    for index in range(2 * HALF):
        put_first(0, index)
    for frame in range(frames):
        for index in range(HALF):
            if frame + 1 < frames:
                for ahead in range(2 * index, 2 * index + 2):
                    put_first(frame + 1, ahead)
            put_second(frame, index)
        if frame == 0:
            fetch.wait()
            load.wait()
        for index in range(HALF):
            put_shifted(s_two[frame], shared_at + index, kept[frame, index].astype(F32))
    copies = []
    for frame in range(frames):
        for index in range(HALF):
            change = product(s_two[frame], w_two, index)
            copies.append(send(outer[frame, index], change, frame, index, held, out, sems))
    for copy in copies:
        copy.wait()


def conv_chunk(info, inner, outer, halo, shared, owners, weights):
    frames, _, cols, chans = outer.shape
    own = cols // owners
    is_outer = shared is not None
    stack = lambda count: pltpu.VMEM((frames, count, cols, 3 * chans), BF16)
    here = pl.BlockSpec(memory_space=pltpu.VMEM)
    there = pl.BlockSpec(memory_space=pltpu.HBM)
    near = lambda v: pltpu.with_memory_space_constraint(v, pltpu.VMEM)
    far = lambda v: pltpu.with_memory_space_constraint(v, pltpu.HBM)
    gain_one, conv_one, gain_two, conv_two = weights
    mixed = pltpu.HBM((owners, frames, HALF, own, chans), BF16)
    keep = pltpu.HBM((frames, HALF, cols, chans), BF16)
    first_rows = (2 if is_outer else 3) * HALF
    new_rows = (1 if is_outer else 2) * HALF
    flops = 2 * frames * (new_rows + HALF) * cols * 9 * chans * chans
    two = [pltpu.VMEM((2 * HALF, cols, 3 * chans), BF16)] * 2 if is_outer else [stack(2 * HALF)]
    return pl.pallas_call(
        outer_body if is_outer else inner_body,
        in_specs=[
            pl.BlockSpec(memory_space=pltpu.SMEM), here, here, there if is_outer else here,
            here, here, here, there,
        ],
        out_specs=[there] if is_outer else [there, there],
        out_shape=[mixed] if is_outer else [mixed, keep],
        scratch_shapes=[
            stack(first_rows),
            *two,
            pltpu.VMEM((frames, HALF, cols, chans), BF16),
            pltpu.VMEM(conv_two.shape, BF16),
            pltpu.VMEM((frames, HALF, owners, own, chans), BF16),
            pltpu.SemaphoreType.DMA((frames,)),
            pltpu.SemaphoreType.DMA,
            pltpu.SemaphoreType.DMA((frames, HALF)),
        ],
        compiler_params=pltpu.CompilerParams(vmem_limit_bytes=28 * 1024 * 1024),
        cost_estimate=pl.CostEstimate(
            flops=flops, bytes_accessed=8 * 1024 * 1024, transcendentals=0
        ),
        name="convs_outer" if is_outer else "convs_inner",
    )(
        info, *((outer, halo, far(shared)) if is_outer else (inner, outer, halo)),
        gain_one, near(conv_one), gain_two, far(conv_two),
    )


def attend_body(group, order, x_ref, gain_three, kernel, gain_four, wq, wk, wv, wo, *refs):
    frames, pixels, chans = x_ref.shape
    count = frames * pixels
    half_three = gain_three[...] * 0.5
    x = x_ref[...].reshape(count, chans).astype(F32)
    third = silu_from_half(scaled(x, half_three)).astype(BF16).reshape(frames, pixels, chans)
    one = jnp.concatenate([third[:1], third[:-1]], axis=0)
    two = jnp.concatenate([third[:1], third[:1], third[:-2]], axis=0)
    taps = jnp.concatenate([two, one, third], axis=-1).reshape(count, 3 * chans)
    timed = x + jnp.dot(taps, kernel[...], preferred_element_type=F32)
    fourth = scaled(timed, gain_four[...]).astype(BF16)
    project = lambda w: jnp.dot(fourth, w[...], preferred_element_type=F32)
    scale = 1.0 / float(chans) ** 0.5
    queries = (project(wq) * scale).astype(BF16).reshape(frames, pixels, chans)
    keys = project(wk).astype(BF16).reshape(frames, pixels, chans)
    values = project(wv).astype(BF16).reshape(frames, pixels, chans)
    size = frames * group
    down = lax.broadcasted_iota(jnp.int32, (size, size), 0)
    along = lax.broadcasted_iota(jnp.int32, (size, size), 1)
    allowed = (down % group == along % group) & (down >= along)
    pieces = []
    for g in range(pixels // group):
        cut = lambda v: v[:, g * group : (g + 1) * group].reshape(size, chans)
        scores = lax.dot_general(
            cut(queries), cut(keys), (((1,), (1,)), ((), ())), preferred_element_type=F32
        )
        scores = jnp.where(allowed, scores, -1e30)
        top = jnp.max(scores, axis=-1, keepdims=True)
        weights = jnp.exp(scores - top)
        total = jnp.sum(weights, axis=-1, keepdims=True)
        weights = (weights * (1.0 / total)).astype(BF16)
        attended = jnp.dot(weights, cut(values), preferred_element_type=F32)
        pieces.append(attended.astype(BF16).reshape(frames, group, chans))
    attended = pieces[0] if len(pieces) == 1 else jnp.concatenate(pieces, axis=1)
    final = timed + jnp.dot(
        attended.reshape(count, chans), wo[...], preferred_element_type=F32
    )
    final = final.astype(BF16).reshape(frames, pixels, chans)
    if len(refs) == 1:
        refs[0][...] = final
        return
    *outs, held = refs
    held[...] = final
    share = frames // len(outs)
    for n, out in enumerate(outs):
        out[...] = held[pl.ds(order[n] * share, share)]


def attend_chunk(x, order, weights, tile, group, members=0):
    frames, pixels, chans = x.shape
    tile = min(tile, pixels)
    near = lambda v: pltpu.with_memory_space_constraint(v, pltpu.VMEM)
    whole = lambda a: pl.BlockSpec(a.shape, lambda p: (0,) * a.ndim)
    count, share = (members, frames // members) if members else (1, frames)
    block = lambda depth: pl.BlockSpec((depth, tile, chans), lambda p: (0, p, 0))
    result = pl.pallas_call(
        functools.partial(attend_body, group),
        grid=(pixels // tile,),
        in_specs=[pl.BlockSpec(memory_space=pltpu.SMEM), block(frames)]
        + [whole(w) for w in weights],
        out_specs=[block(share)] * count,
        out_shape=[pltpu.HBM((share, pixels, chans), BF16)] * count,
        scratch_shapes=[pltpu.VMEM((frames, tile, chans), BF16)] if members else [],
        compiler_params=pltpu.CompilerParams(vmem_limit_bytes=32 * 1024 * 1024),
        cost_estimate=pl.CostEstimate(
            flops=2 * frames * pixels * chans * chans * 9,
            bytes_accessed=4 * 1024 * 1024,
            transcendentals=0,
        ),
        name="attend",
    )(order, x, *[w if w.shape[0] == 1 else near(w) for w in weights])
    return result if members else result[0]


def place_body(count, where, *refs):
    pieces, (out, sems) = refs[:count], refs[-2:]
    if count == 1:
        pieces = [(n, pieces[0].at[n]) for n in range(pieces[0].shape[0])]
    else:
        pieces = [(where[1 + n], piece) for n, piece in enumerate(pieces)]
    rows, own = pieces[0][1].shape[1:3]
    copies = []
    for n, (member, piece) in enumerate(pieces):
        columns = pl.ds(pl.multiple_of(member * own, own), own)
        copies.append(
            pltpu.make_async_copy(piece, out.at[:, pl.ds(where[0], rows), columns], sems.at[n])
        )
    for copy in copies:
        copy.start()
    for copy in copies:
        copy.wait()


def place(where, pieces, shape, result=None):
    here = pl.BlockSpec(memory_space=pltpu.VMEM)
    there = pl.BlockSpec(memory_space=pltpu.HBM)
    scalars = pl.BlockSpec(memory_space=pltpu.SMEM)
    given = [] if result is None else [result]
    return pl.pallas_call(
        functools.partial(place_body, len(pieces)),
        in_specs=[scalars] + [here] * len(pieces) + [there] * len(given),
        out_specs=there,
        out_shape=pltpu.HBM(shape, BF16),
        input_output_aliases={1 + len(pieces): 0} if given else {},
        scratch_shapes=[pltpu.SemaphoreType.DMA((where.shape[0],))],
        compiler_params=pltpu.CompilerParams(vmem_limit_bytes=16 * 1024 * 1024),
        cost_estimate=pl.CostEstimate(
            flops=0, bytes_accessed=2 * 1024 * 1024, transcendentals=0
        ),
        name="place",
    )(where, *[pltpu.with_memory_space_constraint(v, pltpu.VMEM) for v in pieces], *given)


def cut_body(start, video, part, sem):
    copy = pltpu.make_async_copy(video.at[:, pl.ds(start[0], HALF)], part, sem)
    copy.start()
    copy.wait()


def cut(start, video):
    frames, rows, cols, chans = video.shape
    return pl.pallas_call(
        cut_body,
        in_specs=[
            pl.BlockSpec(memory_space=pltpu.SMEM), pl.BlockSpec(memory_space=pltpu.HBM),
        ],
        out_specs=pl.BlockSpec(memory_space=pltpu.VMEM),
        out_shape=pltpu.VMEM((frames, HALF, cols, chans), BF16),
        scratch_shapes=[pltpu.SemaphoreType.DMA],
        compiler_params=pltpu.CompilerParams(vmem_limit_bytes=8 * 1024 * 1024),
        cost_estimate=pl.CostEstimate(
            flops=0, bytes_accessed=2 * 1024 * 1024, transcendentals=0
        ),
        name="cut",
    )(start, pltpu.with_memory_space_constraint(video, pltpu.HBM))


def shards(
    video,
    gain_one,
    conv_one,
    gain_two,
    conv_two,
    gain_three,
    time_kernel,
    gain_four,
    query_weight,
    key_weight,
    value_weight,
    out_weight,
):
    owners = lax.axis_size("tm")
    strips = lax.axis_size("strip")
    strip = lax.axis_index("strip")
    chans = video.shape[-1]
    odd = strip % 2
    siblings = [(i, i ^ 1) for i in range(strips)]
    neighbours = [(i, i + 1 if i % 2 else i - 1) for i in range(1, strips - 1)]
    inner_start = HALF - HALF * odd
    outer_start = HALF * odd
    goes_on = (strip > 0) & (strip < strips - 1)
    info = jnp.stack([odd, goes_on.astype(jnp.int32)])
    row = lambda gain: gain.reshape(1, chans)
    flat = lambda w: w.reshape(-1, chans)
    conv_weights = (row(gain_one), flat(conv_one), row(gain_two), flat(conv_two))
    attend_weights = (
        row(gain_three), flat(time_kernel), row(gain_four),
        query_weight, key_weight, value_weight, out_weight,
    )
    starts = jnp.stack([inner_start, outer_start])
    outer = cut(starts[1:], video)
    from_outer = lax.ppermute(outer, "strip", neighbours)
    inner = cut(starts[:1], video)
    from_sibling = lax.ppermute(inner, "strip", siblings)

    me = lax.axis_index("tm")
    sides = owners // 2
    steps = [(0, 0), (2, 1), (1, 1), (3, 1), (2, 0), (0, 1), (1, 0), (3, 0)]
    member = lambda i, dy, dx: (i // 2 + dy) % sides * 2 + (i + dx) % 2
    to = jnp.stack([member(me, dy, dx) for dy, dx in steps])
    source = jnp.stack([member(me, sides - dy, dx) for dy, dx in steps])
    exchange = lambda v: lax.all_to_all(v, "tm", split_axis=0, concat_axis=0, tiled=True)

    mixed, shared = conv_chunk(info, inner, outer, from_sibling, None, owners, conv_weights)
    block = exchange(mixed)
    by_frame = (owners * block.shape[1], -1, chans)
    final = attend_chunk(block.reshape(by_frame), to, attend_weights, 128, 16)
    (mixed,) = conv_chunk(info, inner, outer, from_outer, shared, owners, conv_weights)
    block = exchange(mixed)
    finals = attend_chunk(block.reshape(by_frame), to, attend_weights, 128, 16, owners)
    back = exchange(final.reshape(block.shape))
    where = jnp.concatenate([starts[1:], source])
    result = place(jnp.broadcast_to(starts[:1], where.shape), [back], video.shape)
    backs = [finals[0]] + [
        lax.ppermute(finals[n], "tm", [(i, member(i, dy, dx)) for i in range(owners)])
        for n, (dy, dx) in enumerate(steps)
        if n
    ]
    backs = [v.reshape(block.shape[1:]) for v in backs]
    return place(where, backs, video.shape, result)


def solution(mesh):
    placed = (P("tm", "strip", None, None), P(), P(), P(), P(), P(), P(), P(), P(), P(), P(), P())
    return jax.shard_map(
        shards, mesh=mesh, in_specs=placed, out_specs=P("tm", "strip", None, None), check_vma=False
    )
```
